32 devices in a mesh: groups: 2 (over y), px: 8 (over z, x), py: 2 (over core).
Axes of the slice: x: 2, y: 2, z: 4, core: 2. Of those that a mesh axis runs over, the one named last changes fastest.
Arguments:
- node_feat: bfloat16 [65536, 128], P(('groups', 'px', 'py')), parts along dimension 0, may hold values from -6 to 6
- edge_feat: bfloat16 [196608, 128], P(('groups', 'px', 'py')), parts along dimension 0, may hold values from -6 to 6
- edge_send: int32 [196608], P(('groups', 'px', 'py')), parts along dimension 0, may hold values from 0 to 2303, as said below
- edge_recv: int32 [196608], P(('groups', 'px', 'py')), parts along dimension 0, may hold values from 0 to 2048, as said below
- halo_send: int32 [64, 128], P(('groups', 'px', 'py')), parts along dimension 0, may hold values from 0 to 2048, as said below
- pool_slot: int32 [65536], P(('groups', 'px', 'py')), parts along dimension 0, may hold values from 0 to 127, as said below
- pool_node: int32 [32, 128], P(('groups', 'px', 'py')), parts along dimension 0, may hold values from 0 to 256, as said below
- coarse_send: int32 [24576], P(('groups', 'px', 'py')), parts along dimension 0, may hold values from 0 to 256, as said below
- coarse_recv: int32 [24576], P(('groups', 'px', 'py')), parts along dimension 0, may hold values from 0 to 256, as said below
- interp_pick: int32 [32, 128], P(('groups', 'px', 'py')), parts along dimension 0, may hold values from 0 to 256, as said below
- interp_slot: int32 [3, 65536], P(None, ('groups', 'px', 'py')), parts along dimension 1, may hold values from 0 to 127, as said below
- interp_wt: float32 [3, 65536], P(None, ('groups', 'px', 'py')), parts along dimension 1, as said below
- edge_in_w: bfloat16 [2, 384, 128], replicated, may hold values from -0.3125 to 0.3125
- pair_in_w: bfloat16 [4, 256, 128], replicated, may hold values from -0.375 to 0.375
- out_w: bfloat16 [6, 128, 128], replicated, may hold values from -0.5 to 0.5
- mlp_vec: float32 [6, 4, 128], replicated
Outputs:
- node_out: bfloat16 [65536, 128], P(('groups', 'px', 'py')), parts along dimension 0
The draws below stay inside these ranges and needn't reach their ends.
There are 2 independent parts, one for each index of `groups`. The reference program is written for one: setup_inputs(seed, part) draws one part's arguments, and reference() takes and returns one part's arrays. A program takes and returns all parts, laid end to end along the dimension named above; an argument that names none is the same for every part. Nothing has to cross between parts.
Inputs may be any that keep to these rules, and one draw needn't show every extreme that they name: `edge_send`: values index a patch's extended table of 2304 rows. On every patch, rows below 5888 name only the patch's own nodes (128 to 2175), and their last 1 to 127 rows are padding with sender 128; the last 256 rows name live rim rows only: lower rim slots below the count the lower neighbour sends, upper rim slots likewise. `edge_recv`: padding rows of a patch's edges have receiver 2048; all others name a node of the patch. `halo_send`: each row holds a ragged count of live rows, then 2048 in the empty slots; counts lie between 64 and 128, and some patch sends a full 128 to a neighbour. Patch 0 sends nothing downward and the last patch nothing upward. `pool_slot`: the slot of a fine node is o * 8 + k with o a patch and k below that patch's number of slots for o (at most 8; some owner gets all 8 slots from every patch). `pool_node`: on patch o, entry p * 8 + k names a coarse node below 256 for the k that patch p uses toward o, and 256 for the others. `coarse_send`: on every patch the last 1 to 127 rows are padding with 256, the others name coarse nodes of that patch. `coarse_recv`: same rows of padding as coarse_send. `interp_pick`: on patch o, entry p * 8 + k names a coarse node for the k below the number of slots that patch p uses from o (at most 8; some owner fills all 8 for every patch), 256 elsewhere. `interp_slot`: each parent's slot is o * 8 + k with o a patch and k below the number of slots that the node's patch uses from o. `interp_wt`: Positive; the three weights of a node sum to one.
All inputs are finite; a program needn't handle non-finite values.
Results may differ from the reference program's by a relative error of at most 0.009.
Values may be sent and summed in bfloat16 or wider, within the bound.
A program may use at most 64 MiB of HBM per device.

```python
import jax
import jax.numpy as jnp
from jax import lax

D = 128
NF = 2048
EF = 6144
EB = 256
H = 128
NC = 256
EC = 768
PC = 8
QC = 8
DEVS = 16


def halo_counts(key):
    key = jax.random.fold_in(key, 101)
    counts = jax.random.randint(key, (DEVS, 2), H // 2, H + 1)
    place = jnp.arange(DEVS)
    sides = jnp.arange(2)
    dead = (place[:, None] == 0) & (sides[None, :] == 0) | (place[:, None] == DEVS - 1) & (sides[None, :] == 1)
    counts = jnp.where(dead, 0, counts)
    chosen = jax.random.randint(jax.random.fold_in(key, 1), (), 1, DEVS - 1)
    side = jax.random.randint(jax.random.fold_in(key, 2), (), 0, 2)
    full = (place[:, None] == chosen) & (sides[None, :] == side)
    return jnp.where(full, H, counts).astype(jnp.int32)


def edge_lists(key):
    counts = halo_counts(key)
    key = jax.random.fold_in(key, 202)
    keys = jax.random.split(key, 4)
    lower = jnp.concatenate([jnp.zeros((1,), jnp.int32), counts[:-1, 1]])
    upper = jnp.concatenate([counts[1:, 0], jnp.zeros((1,), jnp.int32)])
    inner = EF - EB
    padding = jax.random.randint(keys[0], (DEVS, 1), 1, min(128, inner // 2))
    row = jnp.arange(EF)[None, :]
    own_send = H + jax.random.randint(keys[1], (DEVS, EF), 0, NF)
    own_recv = jax.random.randint(keys[2], (DEVS, EF), 0, NF)
    pick = jax.random.randint(keys[3], (DEVS, EF), 0, (lower + upper)[:, None])
    rim_send = jnp.where(pick < lower[:, None], pick, H + NF + pick - lower[:, None])
    on_rim = row >= inner
    padded = (row >= inner - padding) & jnp.logical_not(on_rim)
    send = jnp.where(on_rim, rim_send, jnp.where(padded, H, own_send))
    recv = jnp.where(padded, NF, own_recv)
    return (send.reshape(-1).astype(jnp.int32), recv.reshape(-1).astype(jnp.int32))


def route_loads(key, salt, capacity):
    key = jax.random.fold_in(key, salt)
    loads = jax.random.randint(key, (DEVS, DEVS), max(1, 2 * capacity // 3), capacity + 1)
    star = jax.random.randint(jax.random.fold_in(key, 1), (), 0, DEVS)
    return jnp.where(jnp.arange(DEVS)[None, :] == star, capacity, loads).astype(jnp.int32)


def owner_lists(key, loads, capacity):
    ids = jax.random.randint(key, (DEVS, DEVS, capacity), 0, NC)
    limit = loads.T
    live = jnp.arange(capacity)[None, None, :] < limit[:, :, None]
    return jnp.where(live, ids, NC).reshape(DEVS, DEVS * capacity).astype(jnp.int32)


def coarse_lists(key):
    key = jax.random.fold_in(key, 505)
    keys = jax.random.split(key, 3)
    send = jax.random.randint(keys[0], (DEVS, EC), 0, NC)
    recv = jax.random.randint(keys[1], (DEVS, EC), 0, NC)
    padding = jax.random.randint(keys[2], (DEVS, 1), 1, min(128, EC // 2))
    row = jnp.arange(EC)[None, :]
    live = row < EC - padding
    return (jnp.where(live, send, NC).reshape(-1).astype(jnp.int32), jnp.where(live, recv, NC).reshape(-1).astype(jnp.int32))


def draw_edge_send(key, part):
    return edge_lists(key)[0]


def draw_edge_recv(key, part):
    return edge_lists(key)[1]


def draw_halo_send(key, part):
    counts = halo_counts(key)
    key = jax.random.fold_in(key, 3)
    rows = jax.random.randint(key, (DEVS, 2, H), 0, NF)
    live = jnp.arange(H)[None, None, :] < counts[:, :, None]
    return jnp.where(live, rows, NF).reshape(2 * DEVS, H).astype(jnp.int32)


def draw_pool_slot(key, part):
    loads = route_loads(key, 303, PC)
    key = jax.random.fold_in(key, 5)
    owner = jax.random.randint(key, (DEVS, NF), 0, DEVS)
    limit = jnp.take_along_axis(loads, owner, axis=1)
    slot = jax.random.randint(jax.random.fold_in(key, 1), (DEVS, NF), 0, limit)
    return (owner * PC + slot).reshape(-1).astype(jnp.int32)


def draw_pool_node(key, part):
    loads = route_loads(key, 303, PC)
    key = jax.random.fold_in(key, 7)
    return owner_lists(key, loads, PC)


def draw_coarse_send(key, part):
    return coarse_lists(key)[0]


def draw_coarse_recv(key, part):
    return coarse_lists(key)[1]


def draw_interp_pick(key, part):
    loads = route_loads(key, 404, QC)
    key = jax.random.fold_in(key, 8)
    return owner_lists(key, loads, QC)


def draw_interp_slot(key, part):
    loads = route_loads(key, 404, QC)
    key = jax.random.fold_in(key, 9)
    owner = jax.random.randint(key, (3, DEVS, NF), 0, DEVS)
    limit = loads[jnp.arange(DEVS)[None, :, None], owner]
    slot = jax.random.randint(jax.random.fold_in(key, 1), (3, DEVS, NF), 0, limit)
    return (owner * QC + slot).reshape(3, DEVS * NF).astype(jnp.int32)


def draw_interp_wt(key, part):
    key = jax.random.fold_in(key, 10)
    raw = jax.random.uniform(key, (3, DEVS * NF), jnp.float32, 0.2, 1.0)
    return raw / jnp.sum(raw, axis=0, keepdims=True)


def draw_mlp_vec(key, part):
    key = jax.random.fold_in(key, 11)
    keys = jax.random.split(key, 3)
    biases = 0.5 * jax.random.normal(keys[0], (6, 2, D), jnp.float32)
    gains = 1.0 + jax.random.uniform(keys[1], (6, 1, D), jnp.float32, -0.4, 0.4)
    shifts = 0.5 * jax.random.normal(keys[2], (6, 1, D), jnp.float32)
    return jnp.concatenate([biases, gains, shifts], axis=1)


def shard_levels(rng, dims, cuts, low, largest):
    factor_of = 1.0
    for axis_at, parts in cuts:
        steps = jax.random.uniform(jax.random.fold_in(jax.random.fold_in(rng, 6), axis_at), (parts,), jnp.float32, low / len(cuts), largest / len(cuts))
        factor_of = factor_of * jnp.repeat(jnp.exp(steps), dims[axis_at] // parts).reshape((-1,) + (1,) * (len(dims) - 1 - axis_at))
    return factor_of


def centred(rng, extent, scale, bound, cuts=(), kind=jnp.bfloat16):
    level = shard_levels(rng, extent, cuts, -0.22, 0.18) if cuts else 1.0
    array = jax.random.normal(rng, extent, jnp.float32) * scale * level
    return jnp.minimum(jnp.maximum(array, -bound), bound).astype(kind)


def setup_inputs(seed: int = 0, part: int = 0) -> dict:
    key_list = jax.random.split(jax.random.key(seed), 17)
    own_keys = jax.random.split(jax.random.fold_in(key_list[16], part), 17)
    return {
        "node_feat": centred(own_keys[0], (DEVS * NF, D), 1.0, 6.0, ((0, 16),)),
        "edge_feat": centred(own_keys[1], (DEVS * EF, D), 1.0, 6.0, ((0, 16),)),
        "edge_send": draw_edge_send(jax.random.fold_in(jax.random.fold_in(key_list[16], part), 71), part),
        "edge_recv": draw_edge_recv(jax.random.fold_in(jax.random.fold_in(key_list[16], part), 71), part),
        "halo_send": draw_halo_send(jax.random.fold_in(jax.random.fold_in(key_list[16], part), 71), part),
        "pool_slot": draw_pool_slot(jax.random.fold_in(jax.random.fold_in(key_list[16], part), 71), part),
        "pool_node": draw_pool_node(jax.random.fold_in(jax.random.fold_in(key_list[16], part), 71), part),
        "coarse_send": draw_coarse_send(jax.random.fold_in(jax.random.fold_in(key_list[16], part), 71), part),
        "coarse_recv": draw_coarse_recv(jax.random.fold_in(jax.random.fold_in(key_list[16], part), 71), part),
        "interp_pick": draw_interp_pick(jax.random.fold_in(jax.random.fold_in(key_list[16], part), 71), part),
        "interp_slot": draw_interp_slot(jax.random.fold_in(jax.random.fold_in(key_list[16], part), 71), part),
        "interp_wt": draw_interp_wt(jax.random.fold_in(jax.random.fold_in(key_list[16], part), 71), part),
        "edge_in_w": centred(key_list[12], (2, 3 * D, D), (3 * D) ** -0.5, 0.3125),
        "pair_in_w": centred(key_list[13], (4, 2 * D, D), (2 * D) ** -0.5, 0.375),
        "out_w": centred(key_list[14], (6, D, D), D ** -0.5, 0.5),
        "mlp_vec": draw_mlp_vec(jax.random.fold_in(key_list[16], 71), part),
    }


def layer_norm(values, gain, shift):
    center = values - lax.optimization_barrier(jnp.mean(values, axis=-1, keepdims=True))
    spread = lax.optimization_barrier(jnp.mean(center * center, axis=-1, keepdims=True))
    return center * lax.rsqrt(spread + 1e-05) * gain + shift

def run_mlp(pieces, weight_in, weight_out, params):
    width = weight_out.shape[0]
    total = params[0]
    for place, piece in enumerate(pieces):
        total = total + jnp.dot(piece, weight_in[place * width:(place + 1) * width], preferred_element_type=jnp.float32)
    hidden = jnp.maximum(total, 0.0).astype(jnp.bfloat16)
    result = jnp.dot(hidden, weight_out, preferred_element_type=jnp.float32) + params[1]
    return layer_norm(result, params[2], params[3])

def with_zero(table):
    return jnp.concatenate([table, jnp.zeros((1, table.shape[1]), table.dtype)], axis=0)

def summed(values, index, count):
    return jax.ops.segment_sum(values.astype(jnp.float32), index, num_segments=count + 1)[:count]

def fine_layer(nodes, edges, senders, receivers, rim_lists, edge_in_w, pair_in_w, out_w, mlp_vec, layer):
    rims = lax.map(lambda item: jnp.take(with_zero(item[0]), item[1], axis=0), (nodes, rim_lists))
    blank = jnp.zeros((1, H, D), jnp.bfloat16)
    lower = jnp.concatenate([blank, rims[:-1, 1]], axis=0)
    upper = jnp.concatenate([rims[1:, 0], blank], axis=0)

    def patch(item):
        own, edge_rows, send_rows, recv_rows, low_rim, high_rim = item
        extended = jnp.concatenate([low_rim, own, high_rim], axis=0)
        source = jnp.take(extended, send_rows, axis=0)
        target = jnp.take(with_zero(own), recv_rows, axis=0)
        change = run_mlp([source, target, edge_rows], edge_in_w[layer], out_w[2 * layer], mlp_vec[2 * layer])
        updated = (edge_rows.astype(jnp.float32) + change).astype(jnp.bfloat16)
        gathered = summed(updated, recv_rows, NF).astype(jnp.bfloat16)
        node_change = run_mlp([own, gathered], pair_in_w[layer], out_w[2 * layer + 1], mlp_vec[2 * layer + 1])
        return ((own.astype(jnp.float32) + node_change).astype(jnp.bfloat16), updated)
    return lax.map(patch, (nodes, edges, senders, receivers, lower, upper))

def reference(node_feat, edge_feat, edge_send, edge_recv, halo_send, pool_slot, pool_node, coarse_send, coarse_recv, interp_pick, interp_slot, interp_wt, edge_in_w, pair_in_w, out_w, mlp_vec):
    patches = DEVS
    senders = edge_send.reshape(patches, EF)
    receivers = edge_recv.reshape(patches, EF)
    rim_lists = halo_send.reshape(patches, 2, H)
    first_nodes, first_edges = fine_layer(node_feat.reshape(patches, NF, D), edge_feat.reshape(patches, EF, D), senders, receivers, rim_lists, edge_in_w, pair_in_w, out_w, mlp_vec, 0)
    slots = lax.map(lambda item: summed(item[0], item[1], patches * PC).astype(jnp.bfloat16), (first_nodes, pool_slot.reshape(patches, NF)))
    arrived = slots.reshape(patches, patches, PC, D).transpose(1, 0, 2, 3).reshape(patches, patches * PC, D)

    def owner(item):
        got, node_list, coarse_senders, coarse_receivers, picks = item
        total = summed(got, node_list, NC)
        center = total - lax.optimization_barrier(jnp.mean(total, axis=-1, keepdims=True))
        spread = lax.optimization_barrier(jnp.mean(center * center, axis=-1, keepdims=True))
        pooled = (center * lax.rsqrt(spread + 1e-05)).astype(jnp.bfloat16)
        table = with_zero(pooled)
        coarse_edges = run_mlp([jnp.take(table, coarse_senders, axis=0), jnp.take(table, coarse_receivers, axis=0)], pair_in_w[2], out_w[4], mlp_vec[4]).astype(jnp.bfloat16)
        coarse_agg = summed(coarse_edges, coarse_receivers, NC).astype(jnp.bfloat16)
        coarse_nodes = (pooled.astype(jnp.float32) + run_mlp([pooled, coarse_agg], pair_in_w[3], out_w[5], mlp_vec[5])).astype(jnp.bfloat16)
        return jnp.take(with_zero(coarse_nodes), picks, axis=0)
    outgoing = lax.map(owner, (arrived, pool_node, coarse_send.reshape(patches, EC), coarse_recv.reshape(patches, EC), interp_pick))
    back = outgoing.reshape(patches, patches, QC, D).transpose(1, 0, 2, 3).reshape(patches, patches * QC, D)

    def lift(item):
        own, table, parents, weights = item
        rows = jnp.take(table, parents, axis=0).astype(jnp.float32)
        mixed = weights[0][:, None] * rows[0] + weights[1][:, None] * rows[1] + weights[2][:, None] * rows[2]
        return (own.astype(jnp.float32) + mixed).astype(jnp.bfloat16)
    parent_rows = interp_slot.reshape(3, patches, NF).transpose(1, 0, 2)
    parent_weights = interp_wt.reshape(3, patches, NF).transpose(1, 0, 2)
    second_nodes = lax.map(lift, (first_nodes, back, parent_rows, parent_weights))
    final_nodes, final_edges = fine_layer(second_nodes, first_edges, senders, receivers, rim_lists, edge_in_w, pair_in_w, out_w, mlp_vec, 1)
    return final_nodes.reshape(patches * NF, D)
```

```python
import functools

import jax
import jax.numpy as jnp
from jax import lax
from jax.experimental import pallas as pl
from jax.experimental.pallas import tpu as pltpu
from jax.sharding import PartitionSpec as P

LANES = 128
NC = 256
SLOT = 8
RIM = 128
BLOCKS = 4
TILE = 1024
BF16 = jnp.bfloat16
F32 = jnp.float32


def dot(a, b):
    return jnp.dot(a, b, preferred_element_type=F32)


def column(row):
    return jnp.broadcast_to(row, (LANES, LANES)).T


def columns(ref, start, count):
    return jnp.concatenate([column(ref[pl.ds(start + i, 1), :]) for i in range(count)], axis=0)


def hot(mask):
    return jnp.where(mask, 1.0, 0.0).astype(BF16)


def hot_rows(col, width):
    lane = lax.broadcasted_iota(jnp.int32, col.shape, 1)
    return jnp.concatenate([hot(col == lane + k) for k in range(0, width, LANES)], axis=1)


def hot_columns(rows, height):
    place = lax.broadcasted_iota(jnp.int32, (height, LANES), 0)
    return jnp.concatenate([hot(place == row) for row in rows], axis=1)


def table_of(nodes_ref):
    part = nodes_ref.shape[0] // BLOCKS
    return jnp.concatenate([nodes_ref[b * part : (b + 1) * part, :] for b in range(BLOCKS)], axis=1)


def pick_rows(table, col):
    part = table.shape[0]
    shift = part.bit_length() - 1
    wide = dot(hot_rows(col & (part - 1), part), table)
    block = col >> shift
    out = jnp.zeros(col.shape, F32)
    for b in range(BLOCKS):
        out = jnp.where(block == b, wide[:, b * LANES : (b + 1) * LANES], out)
    return out.astype(BF16)


def normed(values):
    center = values - jnp.mean(values, axis=-1, keepdims=True)
    spread = jnp.mean(center * center, axis=-1, keepdims=True)
    return center * lax.rsqrt(spread + 1e-05)


def run_mlp(pieces, weights, out_w, vec, i):
    both = jnp.concatenate(pieces, axis=1)
    total = dot(both, weights) + vec[i, 0:1, :]
    hidden = jnp.maximum(total, 0.0).astype(BF16)
    result = dot(hidden, out_w[i]) + vec[i, 1:2, :]
    return normed(result) * vec[i, 2:3, :] + vec[i, 3:4, :]


def kernel(
    node,
    edge,
    send,
    recv,
    halo,
    pslot,
    pnode,
    csend,
    crecv,
    ipick,
    islot,
    iwt,
    edge_w,
    pair_w,
    out_w,
    vec,
    out,
    scol,
    rcol,
    e1,
    h1,
    h2,
    acc,
    rim_out,
    rims,
    slots,
    arrived,
    picks,
    back,
    rim_sem,
    pool_sem,
    back_sem,
):
    py = lax.axis_size("py")
    peers = lax.axis_size("px") * py
    me = lax.axis_index("px") * py + lax.axis_index("py")
    nf = node.shape[0]
    ef = edge.shape[0]
    part = nf // BLOCKS
    tiles = ef // TILE
    rows = TILE // LANES
    eb = 2 * RIM

    def place(q):
        return {"px": q // py, "py": lax.rem(q, py)}

    barrier = pltpu.get_barrier_semaphore()

    def greet(d, carry):
        pl.semaphore_signal(
            barrier,
            inc=1,
            device_id=place(lax.rem(me + d, peers)),
            device_id_type=pl.DeviceIdType.MESH,
        )
        return carry

    lax.fori_loop(1, peers, greet, 0)

    def rim_copy(layer, side):
        other = me + (1 if side else -1)
        return pltpu.make_async_remote_copy(
            src_ref=rim_out.at[layer, side],
            dst_ref=rims.at[layer, 1 - side],
            send_sem=rim_sem.at[0, layer, side],
            recv_sem=rim_sem.at[1, layer, 1 - side],
            device_id=place(jnp.clip(other, 0, peers - 1)),
            device_id_type=pl.DeviceIdType.MESH,
        )

    def send_rims(layer, table):
        for side in range(2):
            rim_out[layer, side] = pick_rows(table, column(halo[side : side + 1, :]))
        if layer == 0:
            pl.semaphore_wait(barrier, peers - 1)
        for side in range(2):
            edge_patch = 0 if side == 0 else peers - 1

            @pl.when(me != edge_patch)
            def _(side=side):
                rim_copy(layer, side).start()

            @pl.when(me == edge_patch)
            def _(side=side):
                rims[layer, side] = jnp.zeros((RIM, LANES), BF16)

    def wait_rims(layer):
        for side in range(2):
            edge_patch = 0 if side == 0 else peers - 1

            @pl.when(me != edge_patch)
            def _(side=side):
                copy = rim_copy(layer, side)
                copy.wait_send()
                pltpu.make_async_remote_copy(
                    src_ref=rim_out.at[layer, side],
                    dst_ref=rims.at[layer, side],
                    send_sem=rim_sem.at[0, layer, side],
                    recv_sem=rim_sem.at[1, layer, side],
                    device_id=place(jnp.clip(me + (1 if side else -1), 0, peers - 1)),
                    device_id_type=pl.DeviceIdType.MESH,
                ).wait_recv()

    def exchange(src, dst, sem, d):
        q = lax.rem(me + d, peers)
        return pltpu.make_async_remote_copy(
            src_ref=src.at[pl.ds(pl.multiple_of(q * SLOT, SLOT), SLOT), :],
            dst_ref=dst.at[pl.ds(pl.multiple_of(me * SLOT, SLOT), SLOT), :],
            send_sem=sem.at[0, d],
            recv_sem=sem.at[1, d],
            device_id=place(q),
            device_id_type=pl.DeviceIdType.MESH,
        )

    def arrival(src, dst, sem, d):
        q = lax.rem(me + peers - d, peers)
        return pltpu.make_async_remote_copy(
            src_ref=src.at[pl.ds(pl.multiple_of(q * SLOT, SLOT), SLOT), :],
            dst_ref=dst.at[pl.ds(pl.multiple_of(q * SLOT, SLOT), SLOT), :],
            send_sem=sem.at[0, d],
            recv_sem=sem.at[1, d],
            device_id=place(q),
            device_id_type=pl.DeviceIdType.MESH,
        )

    def all_to_all(src, dst, sem):
        def start(d, carry):
            exchange(src, dst, sem, d).start()
            return carry

        def finish(d, carry):
            exchange(src, dst, sem, d).wait_send()
            arrival(src, dst, sem, d).wait_recv()
            return carry

        lax.fori_loop(1, peers, start, 0)
        mine = pl.ds(pl.multiple_of(me * SLOT, SLOT), SLOT)
        dst[mine, :] = src[mine, :]
        lax.fori_loop(1, peers, finish, 0)

    def fine_layer(layer, nodes, edges, new_edges, new_nodes):
        table = table_of(nodes)
        send_rims(layer, table)
        acc[...] = jnp.zeros(acc.shape, F32)

        def edge_tile(t, last):
            at = pl.ds(pl.multiple_of(t * TILE, TILE), TILE)
            if layer == 0:
                to = columns(recv, t * rows, rows)
                of = columns(send, t * rows, rows)
                rcol[at, :] = to
                scol[at, :] = of
            else:
                to = rcol[at, :]
                of = scol[at, :]
            tab = table_of(nodes)
            source = pick_rows(tab, of - RIM)
            if last:
                tail = of[TILE - eb :]
                rim_row = jnp.where(tail < RIM, tail, tail - nf)
                rim = jnp.concatenate([rims[layer, 0], rims[layer, 1]], axis=0)
                more = dot(hot_rows(rim_row, eb), rim).astype(BF16)
                source = jnp.concatenate([source[: TILE - eb], more], axis=0)
            target = pick_rows(tab, to)
            old = edges[at, :]
            change = run_mlp([source, target, old], edge_w[layer], out_w, vec, 2 * layer)
            new = (old.astype(F32) + change).astype(BF16)
            if new_edges is not None:
                new_edges[at, :] = new
            block = to >> (part.bit_length() - 1)
            none = jnp.zeros_like(new)
            spread = jnp.concatenate(
                [
                    jnp.where(block == b, new.astype(F32), 0.0).astype(BF16)
                    for b in range(BLOCKS)
                ],
                axis=1,
            )
            lists = [recv[pl.ds(t * rows + i, 1), :] & (part - 1) for i in range(rows)]
            acc[...] += dot(hot_columns(lists, part), spread)

        def body(t, carry):
            edge_tile(t, False)
            return carry

        lax.fori_loop(0, tiles - 1, body, 0)
        wait_rims(layer)
        edge_tile(tiles - 1, True)

        for b in range(BLOCKS):
            own = nodes[b * part : (b + 1) * part, :]
            got = acc[:, b * LANES : (b + 1) * LANES].astype(BF16)
            change = run_mlp([own, got], pair_w[layer], out_w, vec, 2 * layer + 1)
            new_nodes[b * part : (b + 1) * part, :] = (own.astype(F32) + change).astype(BF16)

    fine_layer(0, node, edge, e1, h1)

    width = slots.shape[0]
    lists = [pslot[i : i + 1, :] for i in range(nf // LANES)]
    slots[...] = dot(hot_columns(lists, width), h1[...]).astype(BF16).astype(F32)
    all_to_all(slots, arrived, pool_sem)
    lists = [pnode[0:1, i : i + LANES] for i in range(0, width, LANES)]
    pooled = normed(dot(hot_columns(lists, NC), arrived[...].astype(BF16))).astype(BF16)
    count = csend.shape[0]
    first = dot(hot_rows(columns(csend, 0, count), NC), pooled).astype(BF16)
    second = dot(hot_rows(columns(crecv, 0, count), NC), pooled).astype(BF16)
    coarse = run_mlp([first, second], pair_w[2], out_w, vec, 4).astype(BF16)
    lists = [crecv[i : i + 1, :] for i in range(count)]
    got = dot(hot_columns(lists, NC), coarse).astype(BF16)
    change = run_mlp([pooled, got], pair_w[3], out_w, vec, 5)
    coarse = (pooled.astype(F32) + change).astype(BF16)
    cols = [column(ipick[0:1, i : i + LANES]) for i in range(0, width, LANES)]
    picks[...] = dot(hot_rows(jnp.concatenate(cols, axis=0), NC), coarse)
    all_to_all(picks, back, back_sem)

    table = back[...].astype(BF16)
    table = jnp.concatenate([table, table], axis=0)
    which = lax.broadcasted_iota(jnp.int32, (width, LANES), 0)
    for i in range(0, nf, LANES):
        mix = jnp.zeros((width, LANES), F32)
        for j in range(3):
            mix += jnp.where(which == islot[j : j + 1, i : i + LANES], iwt[j : j + 1, i : i + LANES], 0.0)
        mix = mix.T
        high = mix.astype(BF16)
        low = (mix - high.astype(F32)).astype(BF16)
        mixed = dot(jnp.concatenate([high, low], axis=1), table)
        h2[i : i + LANES, :] = (h1[i : i + LANES, :].astype(F32) + mixed).astype(BF16)

    fine_layer(1, h2, e1, None, out)


def per_device(
    node_feat,
    edge_feat,
    edge_send,
    edge_recv,
    halo_send,
    pool_slot,
    pool_node,
    coarse_send,
    coarse_recv,
    interp_pick,
    interp_slot,
    interp_wt,
    edge_in_w,
    pair_in_w,
    out_w,
    mlp_vec,
):
    nf, width = node_feat.shape
    ef = edge_feat.shape[0]
    slots = pool_node.shape[1]
    peers = slots // SLOT
    vmem = pl.BlockSpec(memory_space=pltpu.VMEM)
    return pl.pallas_call(
        kernel,
        out_shape=jax.ShapeDtypeStruct((nf, width), BF16),
        in_specs=[vmem] * 16,
        out_specs=vmem,
        scratch_shapes=[
            pltpu.VMEM((ef, LANES), jnp.int32),
            pltpu.VMEM((ef, LANES), jnp.int32),
            pltpu.VMEM((ef, width), BF16),
            pltpu.VMEM((nf, width), BF16),
            pltpu.VMEM((nf, width), BF16),
            pltpu.VMEM((nf // BLOCKS, BLOCKS * width), F32),
            pltpu.VMEM((2, 2, RIM, width), BF16),
            pltpu.VMEM((2, 2, RIM, width), BF16),
            pltpu.VMEM((slots, width), F32),
            pltpu.VMEM((slots, width), F32),
            pltpu.VMEM((slots, width), F32),
            pltpu.VMEM((slots, width), F32),
            pltpu.SemaphoreType.DMA((2, 2, 2)),
            pltpu.SemaphoreType.DMA((2, peers)),
            pltpu.SemaphoreType.DMA((2, peers)),
        ],
        compiler_params=pltpu.CompilerParams(
            collective_id=0, has_side_effects=True, vmem_limit_bytes=56 * 1024 * 1024
        ),
    )(
        node_feat,
        edge_feat,
        edge_send.reshape(-1, LANES),
        edge_recv.reshape(-1, LANES),
        halo_send,
        pool_slot.reshape(-1, LANES),
        pool_node,
        coarse_send.reshape(-1, LANES),
        coarse_recv.reshape(-1, LANES),
        interp_pick,
        interp_slot,
        interp_wt,
        edge_in_w,
        pair_in_w,
        out_w,
        mlp_vec,
    )


def solution(mesh):
    rows = ("groups", "px", "py")
    placed = (
        P(rows, None),
        P(rows, None),
        P(rows),
        P(rows),
        P(rows, None),
        P(rows),
        P(rows, None),
        P(rows),
        P(rows),
        P(rows, None),
        P(None, rows),
        P(None, rows),
        P(),
        P(),
        P(),
        P(),
    )
    return jax.shard_map(
        per_device,
        mesh=mesh,
        in_specs=placed,
        out_specs=P(rows, None),
        check_vma=False,
    )
```

```python
import functools

import jax
import jax.numpy as jnp
from jax import lax
from jax.experimental import pallas as pl
from jax.experimental.pallas import tpu as pltpu
from jax.sharding import PartitionSpec as P

LANES = 128
NC = 256
SLOT = 8
RIM = 128
BLOCKS = 4
TILE = 2048
BF16 = jnp.bfloat16
F32 = jnp.float32


def dot(a, b):
    return jnp.dot(a, b, preferred_element_type=F32)


def column(row):
    return jnp.broadcast_to(row, (LANES, LANES)).T


def columns(ref, start, count):
    return jnp.concatenate([column(ref[pl.ds(start + i, 1), :]) for i in range(count)], axis=0)


def hot(mask):
    return jnp.where(mask, 1.0, 0.0).astype(BF16)


def hot_rows(col, width):
    lane = lax.broadcasted_iota(jnp.int32, col.shape, 1)
    return jnp.concatenate([hot(col == lane + k) for k in range(0, width, LANES)], axis=1)


def hot_columns(rows, height):
    place = lax.broadcasted_iota(jnp.int32, (height, LANES), 0)
    return jnp.concatenate([hot(place == row) for row in rows], axis=1)


def table_of(nodes_ref):
    part = nodes_ref.shape[0] // BLOCKS
    return jnp.concatenate([nodes_ref[b * part : (b + 1) * part, :] for b in range(BLOCKS)], axis=1)


def pick_rows(table, col):
    part = table.shape[0]
    shift = part.bit_length() - 1
    wide = dot(hot_rows(col & (part - 1), part), table)
    block = col >> shift
    out = jnp.zeros(col.shape, F32)
    for b in range(BLOCKS):
        out = jnp.where(block == b, wide[:, b * LANES : (b + 1) * LANES], out)
    return out.astype(BF16)


def normed(values):
    center = values - jnp.mean(values, axis=-1, keepdims=True)
    spread = jnp.mean(center * center, axis=-1, keepdims=True)
    return center * lax.rsqrt(spread + 1e-05)


def run_mlp(pieces, weights, out_w, vec, i):
    both = jnp.concatenate(pieces, axis=1)
    total = dot(both, weights) + vec[i, 0:1, :]
    hidden = jnp.maximum(total, 0.0).astype(BF16)
    result = dot(hidden, out_w[i]) + vec[i, 1:2, :]
    return normed(result) * vec[i, 2:3, :] + vec[i, 3:4, :]


def kernel(
    node,
    edge,
    send,
    recv,
    halo,
    pslot,
    pnode,
    csend,
    crecv,
    ipick,
    islot,
    iwt,
    edge_w,
    pair_w,
    out_w,
    vec,
    out,
    scol,
    rcol,
    e1,
    h1,
    h2,
    acc,
    rim_out,
    rims,
    slots,
    arrived,
    picks,
    back,
    c_of,
    c_to,
    c_sum,
    mixes,
    rim_sem,
    pool_sem,
    back_sem,
):
    py = lax.axis_size("py")
    peers = lax.axis_size("px") * py
    me = lax.axis_index("px") * py + lax.axis_index("py")
    nf = node.shape[0]
    ef = edge.shape[0]
    part = nf // BLOCKS
    tiles = ef // TILE
    rows = TILE // LANES
    eb = 2 * RIM

    def place(q):
        return {"px": q // py, "py": lax.rem(q, py)}

    barrier = pltpu.get_barrier_semaphore()

    def greet(d, carry):
        pl.semaphore_signal(
            barrier,
            inc=1,
            device_id=place(lax.rem(me + d, peers)),
            device_id_type=pl.DeviceIdType.MESH,
        )
        return carry

    lax.fori_loop(1, peers, greet, 0)

    def rim_copy(layer, side):
        other = me + (1 if side else -1)
        return pltpu.make_async_remote_copy(
            src_ref=rim_out.at[layer, side],
            dst_ref=rims.at[layer, 1 - side],
            send_sem=rim_sem.at[0, layer, side],
            recv_sem=rim_sem.at[1, layer, 1 - side],
            device_id=place(jnp.clip(other, 0, peers - 1)),
            device_id_type=pl.DeviceIdType.MESH,
        )

    def send_rims(layer, nodes):
        table = table_of(nodes)
        for side in range(2):
            rim_out[layer, side] = pick_rows(table, column(halo[side : side + 1, :]))
        if layer == 0:
            pl.semaphore_wait(barrier, peers - 1)
        for side in range(2):
            edge_patch = 0 if side == 0 else peers - 1

            @pl.when(me != edge_patch)
            def _(side=side):
                rim_copy(layer, side).start()

            @pl.when(me == edge_patch)
            def _(side=side):
                rims[layer, side] = jnp.zeros((RIM, LANES), BF16)

    def wait_rims(layer):
        for side in range(2):
            edge_patch = 0 if side == 0 else peers - 1

            @pl.when(me != edge_patch)
            def _(side=side):
                copy = rim_copy(layer, side)
                copy.wait_send()
                pltpu.make_async_remote_copy(
                    src_ref=rim_out.at[layer, side],
                    dst_ref=rims.at[layer, side],
                    send_sem=rim_sem.at[0, layer, side],
                    recv_sem=rim_sem.at[1, layer, side],
                    device_id=place(jnp.clip(me + (1 if side else -1), 0, peers - 1)),
                    device_id_type=pl.DeviceIdType.MESH,
                ).wait_recv()

    def exchange(src, dst, sem, d):
        q = lax.rem(me + d, peers)
        return pltpu.make_async_remote_copy(
            src_ref=src.at[pl.ds(pl.multiple_of(q * SLOT, SLOT), SLOT), :],
            dst_ref=dst.at[pl.ds(pl.multiple_of(me * SLOT, SLOT), SLOT), :],
            send_sem=sem.at[0, d],
            recv_sem=sem.at[1, d],
            device_id=place(q),
            device_id_type=pl.DeviceIdType.MESH,
        )

    def arrival(src, dst, sem, d):
        q = lax.rem(me + peers - d, peers)
        return pltpu.make_async_remote_copy(
            src_ref=src.at[pl.ds(pl.multiple_of(q * SLOT, SLOT), SLOT), :],
            dst_ref=dst.at[pl.ds(pl.multiple_of(q * SLOT, SLOT), SLOT), :],
            send_sem=sem.at[0, d],
            recv_sem=sem.at[1, d],
            device_id=place(q),
            device_id_type=pl.DeviceIdType.MESH,
        )

    def all_to_all(src, dst, sem, meanwhile):
        def start(d, carry):
            exchange(src, dst, sem, d).start()
            return carry

        def finish(d, carry):
            exchange(src, dst, sem, d).wait_send()
            arrival(src, dst, sem, d).wait_recv()
            return carry

        lax.fori_loop(1, peers, start, 0)
        mine = pl.ds(pl.multiple_of(me * SLOT, SLOT), SLOT)
        dst[mine, :] = src[mine, :]
        result = meanwhile()
        lax.fori_loop(1, peers, finish, 0)
        return result

    def fine_layer(layer, nodes, edges, new_edges, new_nodes):
        if layer:
            send_rims(layer, nodes)
        acc[...] = jnp.zeros(acc.shape, F32)

        def edge_tile(t, last):
            at = pl.ds(pl.multiple_of(t * TILE, TILE), TILE)
            if layer == 0:
                to = columns(recv, t * rows, rows)
                of = columns(send, t * rows, rows)
                rcol[at, :] = to
                scol[at, :] = of
            else:
                to = rcol[at, :]
                of = scol[at, :]
            tab = table_of(nodes)
            source = pick_rows(tab, (of[: TILE - eb] if last else of) - RIM)
            if last:
                tail = of[TILE - eb :]
                rim_row = jnp.where(tail < RIM, tail, tail - nf)
                rim = jnp.concatenate([rims[layer, 0], rims[layer, 1]], axis=0)
                more = dot(hot_rows(rim_row, eb), rim).astype(BF16)
                source = jnp.concatenate([source, more], axis=0)
            target = pick_rows(tab, to)
            old = edges[at, :]
            change = run_mlp([source, target, old], edge_w[layer], out_w, vec, 2 * layer)
            new = (old.astype(F32) + change).astype(BF16)
            if new_edges is not None:
                new_edges[at, :] = new
            block = to >> (part.bit_length() - 1)
            spread = jnp.concatenate(
                [
                    jnp.where(block == b, new.astype(F32), 0.0).astype(BF16)
                    for b in range(BLOCKS)
                ],
                axis=1,
            )
            lists = [recv[pl.ds(t * rows + i, 1), :] & (part - 1) for i in range(rows)]
            acc[...] += dot(hot_columns(lists, part), spread)

        def body(t, carry):
            if layer == 0:
                pl.when(t == (tiles - 1) // 2)(lambda: send_rims(layer, nodes))
            edge_tile(t, False)
            return carry

        lax.fori_loop(0, tiles - 1, body, 0)
        wait_rims(layer)
        edge_tile(tiles - 1, True)

        for b in range(BLOCKS):
            own = nodes[b * part : (b + 1) * part, :]
            got = acc[:, b * LANES : (b + 1) * LANES].astype(BF16)
            change = run_mlp([own, got], pair_w[layer], out_w, vec, 2 * layer + 1)
            new_nodes[b * part : (b + 1) * part, :] = (own.astype(F32) + change).astype(BF16)

    fine_layer(0, node, edge, e1, h1)

    width = slots.shape[0]
    lists = [pslot[i : i + 1, :] for i in range(nf // LANES)]
    slots[...] = dot(hot_columns(lists, width), h1[...]).astype(BF16).astype(F32)
    count = csend.shape[0]

    def coarse_lists():
        c_of[...] = hot_rows(columns(csend, 0, count), NC)
        c_to[...] = hot_rows(columns(crecv, 0, count), NC)
        c_sum[...] = hot_columns([crecv[i : i + 1, :] for i in range(count)], NC)

    all_to_all(slots, arrived, pool_sem, coarse_lists)
    lists = [pnode[0:1, i : i + LANES] for i in range(0, width, LANES)]
    pooled = normed(dot(hot_columns(lists, NC), arrived[...].astype(BF16))).astype(BF16)
    first = dot(c_of[...], pooled).astype(BF16)
    second = dot(c_to[...], pooled).astype(BF16)
    coarse = run_mlp([first, second], pair_w[2], out_w, vec, 4).astype(BF16)
    got = dot(c_sum[...], coarse).astype(BF16)
    change = run_mlp([pooled, got], pair_w[3], out_w, vec, 5)
    coarse = (pooled.astype(F32) + change).astype(BF16)
    cols = [column(ipick[0:1, i : i + LANES]) for i in range(0, width, LANES)]
    picks[...] = dot(hot_rows(jnp.concatenate(cols, axis=0), NC), coarse)
    which = lax.broadcasted_iota(jnp.int32, (width, LANES), 0)

    def parent_weights():
        for i in range(0, nf, LANES):
            mix = jnp.zeros((width, LANES), F32)
            for j in range(3):
                parent = islot[j : j + 1, i : i + LANES]
                mix += jnp.where(which == parent, iwt[j : j + 1, i : i + LANES], 0.0)
            mix = mix.T
            high = mix.astype(BF16)
            low = (mix - high.astype(F32)).astype(BF16)
            mixes[i : i + LANES, :] = jnp.concatenate([high, low], axis=1)

    all_to_all(picks, back, back_sem, parent_weights)
    table = back[...].astype(BF16)
    mixed = dot(mixes[...], jnp.concatenate([table, table], axis=0))
    h2[...] = (h1[...].astype(F32) + mixed).astype(BF16)

    fine_layer(1, h2, e1, None, out)


def per_device(
    node_feat,
    edge_feat,
    edge_send,
    edge_recv,
    halo_send,
    pool_slot,
    pool_node,
    coarse_send,
    coarse_recv,
    interp_pick,
    interp_slot,
    interp_wt,
    edge_in_w,
    pair_in_w,
    out_w,
    mlp_vec,
):
    nf, width = node_feat.shape
    ef = edge_feat.shape[0]
    slots = pool_node.shape[1]
    peers = slots // SLOT
    vmem = pl.BlockSpec(memory_space=pltpu.VMEM)
    return pl.pallas_call(
        kernel,
        out_shape=jax.ShapeDtypeStruct((nf, width), BF16),
        in_specs=[vmem] * 16,
        out_specs=vmem,
        scratch_shapes=[
            pltpu.VMEM((ef, LANES), jnp.int32),
            pltpu.VMEM((ef, LANES), jnp.int32),
            pltpu.VMEM((ef, width), BF16),
            pltpu.VMEM((nf, width), BF16),
            pltpu.VMEM((nf, width), BF16),
            pltpu.VMEM((nf // BLOCKS, BLOCKS * width), F32),
            pltpu.VMEM((2, 2, RIM, width), BF16),
            pltpu.VMEM((2, 2, RIM, width), BF16),
            pltpu.VMEM((slots, width), F32),
            pltpu.VMEM((slots, width), F32),
            pltpu.VMEM((slots, width), F32),
            pltpu.VMEM((slots, width), F32),
            pltpu.VMEM((coarse_send.shape[0], NC), BF16),
            pltpu.VMEM((coarse_send.shape[0], NC), BF16),
            pltpu.VMEM((NC, coarse_send.shape[0]), BF16),
            pltpu.VMEM((nf, 2 * slots), BF16),
            pltpu.SemaphoreType.DMA((2, 2, 2)),
            pltpu.SemaphoreType.DMA((2, peers)),
            pltpu.SemaphoreType.DMA((2, peers)),
        ],
        compiler_params=pltpu.CompilerParams(
            collective_id=0, has_side_effects=True, vmem_limit_bytes=56 * 1024 * 1024
        ),
    )(
        node_feat,
        edge_feat,
        edge_send.reshape(-1, LANES),
        edge_recv.reshape(-1, LANES),
        halo_send,
        pool_slot.reshape(-1, LANES),
        pool_node,
        coarse_send.reshape(-1, LANES),
        coarse_recv.reshape(-1, LANES),
        interp_pick,
        interp_slot,
        interp_wt,
        edge_in_w,
        pair_in_w,
        out_w,
        mlp_vec,
    )


def solution(mesh):
    rows = ("groups", "px", "py")
    placed = (
        P(rows, None),
        P(rows, None),
        P(rows),
        P(rows),
        P(rows, None),
        P(rows),
        P(rows, None),
        P(rows),
        P(rows),
        P(rows, None),
        P(None, rows),
        P(None, rows),
        P(),
        P(),
        P(),
        P(),
    )
    return jax.shard_map(
        per_device,
        mesh=mesh,
        in_specs=placed,
        out_specs=P(rows, None),
        check_vma=False,
    )
```
